32 devices in a mesh: row: 8 (over z, x), col: 4 (over y, core).
Axes of the slice: x: 2, y: 2, z: 4, core: 2. Of those that a mesh axis runs over, the one named last changes fastest.
Arguments:
- object_field: float32 [2, 2048, 4096], P(None, 'row', 'col'), may hold values from -4.2 to 4.2
- probe: float32 [2, 128, 128], replicated, may hold values from -4.2 to 4.2
- position: int32 [8, 4, 48, 2], P('row', 'col'), may hold values from 0 to 1023, as said below
- live_count: int32 [8, 4], P('row', 'col'), may hold values from 1 to 48, as said below
- intensity: float32 [8, 4, 48, 128, 128], P('row', 'col'), may hold values from 0 to 3
Outputs:
- object_out: float32 [2, 2048, 4096], P(None, 'row', 'col')
- probe_out: float32 [2, 128, 128], replicated
The draws below stay inside these ranges and needn't reach their ends.
Inputs may be any that keep to these rules, and one draw needn't show every extreme that they name: `position`: every patch lies inside the object: tiles of the last row have first rows up to 128, tiles of the last column first columns up to 896. Slots 0 to live_count - 1 of a tile are live; in every draw some tile has all 48 slots live.
All inputs are finite; a program needn't handle non-finite values.
Results may differ from the reference program's by a relative error of at most 0.0003.
Values sent between devices are 32-bit elements; how exact they have to be, the bound alone decides.
A program may use at most 128 MiB of HBM per device.

```python
import math
import jax
import jax.numpy as jnp
from jax import lax

PATCH = 128
RD = 256
CD = 1024
CAP = 48
ITERS = 2
TR = 8
TC = 4
NR = 2048
NC = 4096


def draw_live_count(key, part):
    key = jax.random.fold_in(key, 11)
    keys = jax.random.split(key, 5)
    pair_count = TR // 2
    busy = jax.random.randint(keys[0], (pair_count, TC), 0, 2)
    forced_pair = jax.random.randint(keys[1], (), 0, pair_count)
    pair_ids = jnp.arange(pair_count, dtype=jnp.int32)[:, None]
    col_ids = jnp.arange(TC, dtype=jnp.int32)[None, :]
    busy = jnp.maximum(busy, ((pair_ids == forced_pair) & (col_ids == 0)).astype(jnp.int32))
    which = jax.random.randint(keys[2], (pair_count, 1, TC), 0, 2)
    member = jnp.arange(2, dtype=jnp.int32)[None, :, None]
    lesser = jax.random.randint(keys[3], (pair_count, 2, TC), 1, CAP // 4 + 1)
    drawn = jax.random.randint(keys[4], (pair_count, 2, TC), 1, CAP // 2 + 1)
    busy_counts = jnp.where(member == which, CAP, lesser)
    counts = jnp.where(busy[:, None, :] == 1, busy_counts, drawn)
    return counts.reshape(TR, TC).astype(jnp.int32)


def draw_position(key, part):
    key = jax.random.fold_in(key, 23)
    keys = jax.random.split(key, 4)
    shape = (TR, TC, CAP)
    row_first = jax.random.randint(keys[0], shape, 0, RD)
    row_edge = jax.random.randint(keys[1], shape, 0, RD - PATCH + 1)
    col_first = jax.random.randint(keys[2], shape, 0, CD)
    col_edge = jax.random.randint(keys[3], shape, 0, CD - PATCH + 1)
    tile_rows = jnp.arange(TR, dtype=jnp.int32)[:, None, None]
    tile_cols = jnp.arange(TC, dtype=jnp.int32)[None, :, None]
    slot_ids = jnp.arange(CAP, dtype=jnp.int32)[None, None, :]
    row_first = jnp.where(tile_rows == TR - 1, row_edge, row_first)
    col_first = jnp.where(tile_cols == TC - 1, col_edge, col_first)
    root = (tile_rows == 0) & (tile_cols == 0)
    row_first = jnp.where(root & (slot_ids == 0), RD - 1, row_first)
    col_first = jnp.where(root & (slot_ids == 0), CD - 1, col_first)
    row_first = jnp.where(root & (slot_ids == 1), 0, row_first)
    col_first = jnp.where(root & (slot_ids == 1), 0, col_first)
    return jnp.stack([row_first, col_first], axis=-1).astype(jnp.int32)


def levels(rng, extent, cuts, low, largest):
    def one(dim, shards_of):
        draws = jax.random.uniform(jax.random.fold_in(jax.random.fold_in(rng, 6), dim), (shards_of,), jnp.float32, low / len(cuts), largest / len(cuts))
        return jnp.repeat(jnp.exp(draws), extent[dim] // shards_of).reshape((-1,) + (1,) * (len(extent) - dim - 1))

    gain = one(*cuts[0])
    for cut in cuts[1:]:
        gain = gain * one(*cut)
    return gain


def noise(rng, dims, spread, bound, pieces=(), kind=jnp.bfloat16):
    factor_of = levels(rng, dims, pieces, -0.22, 0.18) if pieces else 1.0
    drawn = jax.random.normal(rng, dims, jnp.float32) * spread * factor_of
    return jnp.minimum(jnp.maximum(drawn, -bound), bound).astype(kind)


def setup_inputs(seed: int = 0) -> dict:
    key_list = jax.random.split(jax.random.key(seed), 6)
    return {
        "object_field": noise(key_list[0], (2, NR, NC), 0.7, 4.2, ((1, 8), (2, 4)), jnp.float32),
        "probe": noise(key_list[1], (2, PATCH, PATCH), 0.7, 4.2, (), jnp.float32),
        "position": draw_position(jax.random.fold_in(key_list[5], 71), 0),
        "live_count": draw_live_count(jax.random.fold_in(key_list[5], 71), 0),
        "intensity": jnp.clip(3.0 * jax.random.uniform(key_list[4], (TR, TC, CAP, PATCH, PATCH), jnp.float32) ** levels(key_list[4], (TR, TC, CAP, PATCH, PATCH), ((0, 8), (1, 4)), -0.2, 0.2), 0.0, 3.0),
    }


FULL_PRECISION = lax.Precision.HIGHEST
STEP_OBJECT = 0.05
STEP_PROBE = 0.25


def fourier_tables(length):
    indices = jnp.arange(length, dtype=jnp.int32)
    product = (indices[:, None] * indices[None, :]) % length
    angles = product.astype(jnp.float32) * (2.0 * math.pi / length)
    return jnp.cos(angles), jnp.sin(angles)


def left_mul(table, stack_in):
    return jnp.einsum("kn,bnm->bkm", table, stack_in, precision=FULL_PRECISION)


def right_mul(stack_in, table):
    return jnp.einsum("bkn,nm->bkm", stack_in, table, precision=FULL_PRECISION)


def transform(real_in, imag_in, cos_table, sin_table, direction):
    left_re = left_mul(cos_table, real_in) - direction * left_mul(sin_table, imag_in)
    left_im = left_mul(cos_table, imag_in) + direction * left_mul(sin_table, real_in)
    out_re = right_mul(left_re, cos_table) - direction * right_mul(left_im, sin_table)
    out_im = right_mul(left_im, cos_table) + direction * right_mul(left_re, sin_table)
    scale = 1.0 / cos_table.shape[0]
    return out_re * scale, out_im * scale


def wave_terms(patches, probe_now, measured, live_mask, cos_table, sin_table):
    obj_re, obj_im = patches[:, 0], patches[:, 1]
    prb_re, prb_im = probe_now[0], probe_now[1]
    psi_re = prb_re * obj_re - prb_im * obj_im
    psi_im = prb_re * obj_im + prb_im * obj_re
    far_re, far_im = transform(psi_re, psi_im, cos_table, sin_table, -1.0)
    power = far_re * far_re + far_im * far_im
    weight = 2.0 * (power - measured) * live_mask[:, None, None]
    back_re, back_im = transform(weight * far_re, weight * far_im, cos_table, sin_table, 1.0)
    grad_re = prb_re * back_re + prb_im * back_im
    grad_im = prb_re * back_im - prb_im * back_re
    probe_re = jnp.sum(obj_re * back_re + obj_im * back_im, axis=0)
    probe_im = jnp.sum(obj_re * back_im - obj_im * back_re, axis=0)
    return jnp.stack([grad_re, grad_im], axis=1), jnp.stack([probe_re, probe_im], axis=0)


def reference(object_field, probe, position, live_count, intensity):
    cos_table, sin_table = fourier_tables(PATCH)
    object_now, probe_now = object_field, probe
    live_total = jnp.sum(live_count).astype(jnp.float32)
    all_live = jnp.ones((1,), jnp.float32)
    zero_start = jnp.int32(0)
    for sweep in range(ITERS):
        def tile_step(tile, carry):
            tile_row = (tile // TC).astype(jnp.int32)
            tile_col = (tile % TC).astype(jnp.int32)
            live_here = live_count[tile_row, tile_col].astype(jnp.int32)

            def slot_step(slot, inner):
                gradient, probe_grad = inner
                row_at = (tile_row * RD + position[tile_row, tile_col, slot, 0]).astype(jnp.int32)
                col_at = (tile_col * CD + position[tile_row, tile_col, slot, 1]).astype(jnp.int32)
                patches = lax.dynamic_slice(object_now, (zero_start, row_at, col_at), (2, PATCH, PATCH))
                measured = intensity[tile_row, tile_col, slot][None]
                grad_patch, grad_probe = wave_terms(patches[None], probe_now, measured, all_live, cos_table, sin_table)
                current = lax.dynamic_slice(gradient, (zero_start, row_at, col_at), (2, PATCH, PATCH))
                gradient = lax.dynamic_update_slice(gradient, current + grad_patch[0], (zero_start, row_at, col_at))
                return gradient, probe_grad + grad_probe

            return lax.fori_loop(jnp.int32(0), live_here, slot_step, carry)

        start = (jnp.zeros_like(object_now), jnp.zeros_like(probe_now))
        gradient, probe_grad = lax.fori_loop(jnp.int32(0), jnp.int32(TR * TC), tile_step, start)
        object_now = object_now - STEP_OBJECT * gradient
        probe_now = probe_now - STEP_PROBE * probe_grad / live_total
    return object_now, probe_now
```

```python
import functools

import jax
import jax.numpy as jnp
import ml_dtypes
import numpy as np
from jax import lax
from jax.experimental import pallas as pl
from jax.experimental.pallas import tpu as pltpu
from jax.sharding import PartitionSpec as P

GROUP = 4
ITERS = 2
STEP_OBJECT = 0.05
STEP_PROBE = 0.25


def shifted(block, axis, distance):
    devices = range(lax.axis_size(axis))
    route = [(i - distance, i) for i in devices if i - distance in devices]
    return lax.ppermute(block, axis, route)


def fourier_tables(length):
    indices = np.arange(length)
    angles = (indices[:, None] * indices[None, :] % length) * (2.0 * np.pi / length)
    cos, sin = np.cos(angles), np.sin(angles)
    table = np.block([[cos, sin], [-sin, cos]])

    def parts(full):
        high = full.astype(ml_dtypes.bfloat16)
        low = (full - high.astype(np.float64)).astype(ml_dtypes.bfloat16)
        return high, low

    return (*parts(table), *parts(table.T / length))


def split(value):
    high = value.astype(jnp.bfloat16)
    low = (value - high.astype(jnp.float32)).astype(jnp.bfloat16)
    return high, low


def mm(a, b):
    return jnp.dot(a, b, preferred_element_type=jnp.float32)


def left(table_high, table_low, value):
    high, low = split(value)
    return mm(table_high, high) + mm(table_high, low) + mm(table_low, high)


def right(value, table_high, table_low):
    high, low = split(value)
    return mm(high, table_high) + mm(low, table_high) + mm(high, table_low)


def slots_kernel(
    live_ref, pos_ref, own, below, beside, prb, a_hi, a_lo, t_hi, t_lo, measured,
    grad, pgrad, ext, values, sems,
):
    strips, _, rows, side = own.shape
    copies = [
        pltpu.make_async_copy(own, ext.at[pl.ds(0, strips), :, pl.ds(0, rows), :], sems.at[0]),
        pltpu.make_async_copy(below, ext.at[pl.ds(0, strips), :, pl.ds(rows, side), :], sems.at[1]),
        pltpu.make_async_copy(beside, ext.at[strips], sems.at[2]),
        pltpu.make_async_copy(measured, values, sems.at[3]),
    ]
    for copy in copies:
        copy.start()
    for strip in range(strips + 1):
        grad[strip] = jnp.zeros(grad.shape[1:], jnp.float32)
    pgrad[...] = jnp.zeros_like(pgrad)
    for copy in copies:
        copy.wait()

    live = live_ref[0]
    lane = lax.broadcasted_iota(jnp.int32, (side, side), 1)

    def block(index, _):
        places = []
        objects = []
        waves = []
        for member in range(GROUP):
            slot = index * GROUP + member
            on = slot < live
            row = jnp.where(on, pos_ref[2 * slot], 0)
            col = jnp.where(on, pos_ref[2 * slot + 1], 0)
            strip = col // side
            shift = col - strip * side
            keep = lane >= shift
            back = (side - shift) % side
            window = pl.ds(row, side)

            def take(part):
                here = ext[strip, part, window, :]
                there = ext[strip + 1, part, window, :]
                return pltpu.roll(jnp.where(keep, here, there), back, 1)

            obj_re, obj_im = take(0), take(1)
            psi_re = prb[0] * obj_re - prb[1] * obj_im
            psi_im = prb[0] * obj_im + prb[1] * obj_re
            places.append((slot, on, strip, shift, window, keep))
            objects.append((obj_re, obj_im))
            waves.append(jnp.concatenate([psi_re, psi_im], axis=1))
        half = right(jnp.concatenate(waves, axis=0), t_hi[...], t_lo[...])
        half = jnp.concatenate(
            [
                jnp.concatenate(
                    [half[m * side : (m + 1) * side, :side] for m in range(GROUP)], axis=1
                ),
                jnp.concatenate(
                    [half[m * side : (m + 1) * side, side:] for m in range(GROUP)], axis=1
                ),
            ],
            axis=0,
        )
        far = left(a_hi[...], a_lo[...], half)
        far_re, far_im = far[:side], far[side:]
        power = far_re * far_re + far_im * far_im
        wanted = jnp.concatenate([values[places[m][0]] for m in range(GROUP)], axis=1)
        scale = jnp.concatenate(
            [
                jnp.full((1, side), jnp.where(places[m][1], 2.0, 0.0), jnp.float32)
                for m in range(GROUP)
            ],
            axis=1,
        )
        weight = scale * (power - wanted)
        chi = jnp.concatenate([weight * far_re, weight * far_im], axis=0)
        half = left(t_hi[...], t_lo[...], chi)
        half = jnp.concatenate(
            [
                jnp.concatenate(
                    [
                        half[:side, m * side : (m + 1) * side],
                        half[side:, m * side : (m + 1) * side],
                    ],
                    axis=1,
                )
                for m in range(GROUP)
            ],
            axis=0,
        )
        near = right(half, a_hi[...], a_lo[...])
        sum_re = jnp.zeros((side, side), jnp.float32)
        sum_im = jnp.zeros((side, side), jnp.float32)
        for member in range(GROUP):
            slot, on, strip, shift, window, keep = places[member]
            obj_re, obj_im = objects[member]
            back_re = near[member * side : (member + 1) * side, :side]
            back_im = near[member * side : (member + 1) * side, side:]
            sum_re += obj_re * back_re + obj_im * back_im
            sum_im += obj_re * back_im - obj_im * back_re
            for part, value in (
                (0, prb[0] * back_re + prb[1] * back_im),
                (1, prb[0] * back_im - prb[1] * back_re),
            ):
                turned = pltpu.roll(value, shift, 1)
                grad[strip, part, window, :] += jnp.where(keep, turned, 0.0)
                grad[strip + 1, part, window, :] += jnp.where(keep, 0.0, turned)
        pgrad[0] += sum_re
        pgrad[1] += sum_im
        return 0

    lax.fori_loop(0, (live + GROUP - 1) // GROUP, block, 0)


def slots_call(live, places, own, below, beside, probe, tables, measured):
    strips, _, rows, side = own.shape
    shape = (strips + 1, 2, rows + side, side)
    smem = pl.BlockSpec(memory_space=pltpu.SMEM)
    vmem = pl.BlockSpec(memory_space=pltpu.VMEM)
    hbm = pl.BlockSpec(memory_space=pl.ANY)
    return pl.pallas_call(
        slots_kernel,
        out_shape=(
            jax.ShapeDtypeStruct(shape, jnp.float32),
            jax.ShapeDtypeStruct(probe.shape, jnp.float32),
        ),
        in_specs=[smem, smem, hbm, hbm, hbm, vmem, vmem, vmem, vmem, vmem, hbm],
        out_specs=(vmem, vmem),
        scratch_shapes=[
            pltpu.VMEM(shape, jnp.float32),
            pltpu.VMEM(measured.shape, jnp.float32),
            pltpu.SemaphoreType.DMA((4,)),
        ],
        compiler_params=pltpu.CompilerParams(vmem_limit_bytes=40 * 1024 * 1024),
    )(live, places, own, below, beside, probe, *tables, measured)


def body(object_field, probe, position, live_count, intensity):
    side = probe.shape[1]
    rows = object_field.shape[1]
    strips = object_field.shape[2] // side
    tables = [jnp.asarray(t) for t in fourier_tables(side)]
    places = position[0, 0].reshape(-1)
    measured = intensity[0, 0]
    live = live_count.reshape(1)
    live_total = lax.psum(live.astype(jnp.float32), ("row", "col"))
    now = object_field.reshape(2, rows, strips, side).transpose(2, 0, 1, 3)
    probe_now = probe
    for sweep in range(ITERS):
        below = shifted(now[:, :, :side, :], "row", -1)
        beside = shifted(jnp.concatenate([now[0], below[0]], axis=1), "col", -1)
        grad, probe_grad = slots_call(
            live, places, now, below, beside, probe_now, tables, measured
        )
        probe_total = lax.psum(probe_grad, ("row", "col"))
        spill = shifted(grad[strips], "col", 1)
        tall = grad[:strips].at[0].add(spill)
        lower = shifted(tall[:, :, rows:, :], "row", 1)
        own_grad = tall[:, :, :rows, :].at[:, :, :side, :].add(lower)
        now = now - STEP_OBJECT * own_grad
        probe_now = probe_now - STEP_PROBE * probe_total / live_total
    return (now.transpose(1, 2, 0, 3).reshape(object_field.shape), probe_now)


def solution(mesh):
    placed = (
        P(None, "row", "col"),
        P(),
        P("row", "col", None, None),
        P("row", "col"),
        P("row", "col", None, None, None),
    )
    return jax.shard_map(
        body, mesh=mesh, in_specs=placed, out_specs=(P(None, "row", "col"), P()), check_vma=False
    )
```

```python
import functools

import jax
import jax.numpy as jnp
import ml_dtypes
import numpy as np
from jax import lax
from jax.experimental import pallas as pl
from jax.experimental.pallas import tpu as pltpu
from jax.sharding import PartitionSpec as P

GROUP = 8
CHAIN = 4
CHUNKS = 4
ITERS = 2
STEP_OBJECT = 0.05
STEP_PROBE = 0.25
MESH = pl.DeviceIdType.MESH


def shifted(block, axis, distance):
    devices = range(lax.axis_size(axis))
    route = [(i - distance, i) for i in devices if i - distance in devices]
    return lax.ppermute(block, axis, route)


def fourier_tables(length):
    indices = np.arange(length)
    angles = (indices[:, None] * indices[None, :] % length) * (2.0 * np.pi / length)
    cos, sin = np.cos(angles), np.sin(angles)
    table = np.block([[cos, sin], [-sin, cos]])

    def parts(full):
        high = full.astype(ml_dtypes.bfloat16)
        low = (full - high.astype(np.float64)).astype(ml_dtypes.bfloat16)
        return high, low

    return (*parts(table), *parts(table.T / length))


def split(value):
    high = value.astype(jnp.bfloat16)
    low = (value - high.astype(jnp.float32)).astype(jnp.bfloat16)
    return high, low


def mm(a, b):
    return jnp.dot(a, b, preferred_element_type=jnp.float32)


def left(table_high, table_low, value):
    high, low = split(value)
    return mm(table_high, high) + mm(table_high, low) + mm(table_low, high)


def right(value, table_high, table_low):
    high, low = split(value)
    return mm(high, table_high) + mm(low, table_high) + mm(high, table_low)


def spectra(waves, wanted, on, a_hi, a_lo, t_hi, t_lo):
    count, side = len(waves), waves[0].shape[0]
    spans = [slice(m * side, (m + 1) * side) for m in range(count)]
    half = right(jnp.concatenate(waves, axis=0), t_hi[...], t_lo[...])
    half = jnp.concatenate(
        [
            jnp.concatenate([half[span, :side] for span in spans], axis=1),
            jnp.concatenate([half[span, side:] for span in spans], axis=1),
        ],
        axis=0,
    )
    far = left(a_hi[...], a_lo[...], half)
    far_re, far_im = far[:side], far[side:]
    power = far_re * far_re + far_im * far_im
    scale = jnp.concatenate(
        [jnp.full((1, side), jnp.where(live, 2.0, 0.0), jnp.float32) for live in on], axis=1
    )
    weight = scale * (power - jnp.concatenate(wanted, axis=1))
    half = left(
        t_hi[...], t_lo[...], jnp.concatenate([weight * far_re, weight * far_im], axis=0)
    )
    half = jnp.concatenate(
        [jnp.concatenate([half[:side, span], half[side:, span]], axis=1) for span in spans],
        axis=0,
    )
    near = right(half, a_hi[...], a_lo[...])
    return [near[span] for span in spans]


def slots_kernel(
    live_ref, pos_ref, own, below, beside, corner, prb, a_hi, a_lo, t_hi, t_lo, measured,
    own_out, down_out, right_out, corner_out, pgrad_out,
    ext, grad, pgrad, values, sems,
):
    _, rows, width = own.shape
    side = prb.shape[1]
    strips = width // side
    top, low = pl.ds(0, rows), pl.ds(rows, side)
    copies = [pltpu.make_async_copy(measured, values, sems.at[0])]
    for strip in range(strips):
        columns = pl.ds(strip * side, side)
        copies.append(
            pltpu.make_async_copy(own.at[:, :, columns], ext.at[strip, :, top, :], sems.at[2 * strip + 1])
        )
        copies.append(
            pltpu.make_async_copy(below.at[:, :, columns], ext.at[strip, :, low, :], sems.at[2 * strip + 2])
        )
    copies.append(
        pltpu.make_async_copy(beside, ext.at[strips, :, top, :], sems.at[2 * strips + 1])
    )
    copies.append(
        pltpu.make_async_copy(corner, ext.at[strips, :, low, :], sems.at[2 * strips + 2])
    )
    for copy in copies:
        copy.start()
    for strip in range(strips + 1):
        grad[strip] = jnp.zeros(grad.shape[1:], jnp.float32)
    pgrad[...] = jnp.zeros_like(pgrad)
    for copy in copies:
        copy.wait()

    live = live_ref[0]
    lane = lax.broadcasted_iota(jnp.int32, (side, side), 1)

    def block(index, _):
        places = []
        objects = []
        waves = []
        for member in range(GROUP):
            slot = index * GROUP + member
            on = slot < live
            row = jnp.where(on, pos_ref[2 * slot], 0)
            col = jnp.where(on, pos_ref[2 * slot + 1], 0)
            strip = col // side
            shift = col - strip * side
            keep = lane >= shift
            back = (side - shift) % side
            window = pl.ds(row, side)

            def take(part):
                here = ext[strip, part, window, :]
                there = ext[strip + 1, part, window, :]
                return pltpu.roll(jnp.where(keep, here, there), back, 1)

            obj_re, obj_im = take(0), take(1)
            psi_re = prb[0] * obj_re - prb[1] * obj_im
            psi_im = prb[0] * obj_im + prb[1] * obj_re
            places.append((slot, on, strip, shift, window, keep))
            objects.append((obj_re, obj_im))
            waves.append(jnp.concatenate([psi_re, psi_im], axis=1))
        near = []
        for first in range(0, GROUP, CHAIN):
            members = slice(first, first + CHAIN)
            near += spectra(waves[members], [values[p[0]] for p in places[members]],
                            [p[1] for p in places[members]], a_hi, a_lo, t_hi, t_lo)
        sum_re = jnp.zeros((side, side), jnp.float32)
        sum_im = jnp.zeros((side, side), jnp.float32)
        for member in range(GROUP):
            slot, on, strip, shift, window, keep = places[member]
            obj_re, obj_im = objects[member]
            back_re, back_im = near[member][:, :side], near[member][:, side:]
            sum_re += obj_re * back_re + obj_im * back_im
            sum_im += obj_re * back_im - obj_im * back_re
            for part, value in (
                (0, prb[0] * back_re + prb[1] * back_im),
                (1, prb[0] * back_im - prb[1] * back_re),
            ):
                turned = pltpu.roll(value, shift, 1)
                grad[strip, part, window, :] += jnp.where(keep, turned, 0.0)
                grad[strip + 1, part, window, :] += jnp.where(keep, 0.0, turned)
        pgrad[0] += sum_re
        pgrad[1] += sum_im
        return 0

    lax.fori_loop(0, (live + GROUP - 1) // GROUP, block, 0)

    pieces, deep, _ = pgrad_out.shape
    per = 2 * side // pieces
    for piece in range(pieces):
        part, start = divmod(piece * per, side)
        pgrad_out[piece, :per] = pgrad[part, start : start + per]
        pgrad_out[piece, per:] = jnp.full((deep - per, side), live.astype(jnp.float32))
    copies = []
    for strip in range(strips):
        ext[strip, :, :rows] -= STEP_OBJECT * grad[strip, :, :rows]
        columns = pl.ds(strip * side, side)
        copies.append(
            pltpu.make_async_copy(grad.at[strip, :, low, :], down_out.at[:, :, columns], sems.at[2 * strip])
        )
        copies.append(
            pltpu.make_async_copy(ext.at[strip, :, top, :], own_out.at[:, :, columns], sems.at[2 * strip + 1])
        )
        copies[-2].start()
        copies[-1].start()
    copies.append(
        pltpu.make_async_copy(grad.at[strips, :, top, :], right_out, sems.at[2 * strips])
    )
    copies.append(
        pltpu.make_async_copy(grad.at[strips, :, low, :], corner_out, sems.at[2 * strips + 1])
    )
    copies[-2].start()
    copies[-1].start()
    for copy in copies:
        copy.wait()


def slots_call(live, places, own, below, beside, corner, probe, tables, measured, pieces):
    _, rows, width = own.shape
    side = probe.shape[1]
    strips = width // side
    shape = (strips + 1, 2, rows + side, side)
    smem = pl.BlockSpec(memory_space=pltpu.SMEM)
    vmem = pl.BlockSpec(memory_space=pltpu.VMEM)
    hbm = pl.BlockSpec(memory_space=pl.ANY)
    sent = (pieces, 2 * side // pieces + 8, side)
    return pl.pallas_call(
        slots_kernel,
        out_shape=[
            jax.ShapeDtypeStruct(of, jnp.float32)
            for of in (own.shape, below.shape, beside.shape, corner.shape, sent)
        ],
        in_specs=[smem, smem, hbm, hbm, hbm, hbm, vmem, vmem, vmem, vmem, vmem, hbm],
        out_specs=[hbm, hbm, hbm, hbm, vmem],
        scratch_shapes=[
            pltpu.VMEM(shape, jnp.float32),
            pltpu.VMEM(shape, jnp.float32),
            pltpu.VMEM(probe.shape, jnp.float32),
            pltpu.VMEM(measured.shape, jnp.float32),
            pltpu.SemaphoreType.DMA((2 * strips + 3,)),
        ],
        compiler_params=pltpu.CompilerParams(vmem_limit_bytes=40 * 1024 * 1024),
    )(live, places, own, below, beside, corner, probe, *tables, measured)


class Mover:
    def __init__(self, sends, recvs):
        self.sends, self.recvs, self.used = sends, recvs, 0

    def make(self, src, dst, peer):
        index, self.used = self.used, self.used + 1
        return pltpu.make_async_remote_copy(
            src_ref=src, dst_ref=dst, send_sem=self.sends.at[index], recv_sem=self.recvs.at[index],
            device_id=peer, device_id_type=MESH,
        )


def exchange_kernel(n_row, n_col, spill, halo, *refs):
    refs = list(refs)
    own = refs.pop(0)
    if spill:
        down, right_rim, far, sent, prb = refs[:5]
        del refs[:5]
    if halo:
        below, beside, corner = refs[:3]
        del refs[:3]
    if spill:
        now, out = refs[:2]
        del refs[:2]
        got_down, got_right, got_far, from_rows, from_cols = refs[:5]
        del refs[:5]
    else:
        now = own
    mover = Mover(*refs)
    _, rows, width = now.shape
    row, col = lax.axis_index("row"), lax.axis_index("col")
    row_peers = [lax.rem(row + d, n_row) for d in range(1, n_row)]
    col_peers = [lax.rem(col + d, n_col) for d in range(1, n_col)]
    next_row, last_row = row_peers[0], row_peers[-1]
    next_col, last_col = col_peers[0], col_peers[-1]
    has_prev_row, has_next_row = row > 0, row < n_row - 1
    has_prev_col, has_next_col = col > 0, col < n_col - 1
    has_prev_far = jnp.logical_and(has_prev_row, has_prev_col)
    has_next_far = jnp.logical_and(has_next_row, has_next_col)

    barrier = pltpu.get_barrier_semaphore()
    greeted = [(peer, col) for peer in row_peers] + [(row, peer) for peer in col_peers]
    greeted += [(next_row, next_col), (last_row, last_col)]
    for peer in greeted:
        pl.semaphore_signal(barrier, inc=1, device_id=peer, device_id_type=MESH)
    pl.semaphore_wait(barrier, len(greeted))

    edge = corner.shape[1] if halo else far.shape[1]
    step = width // CHUNKS
    spans = [pl.ds(c * step, step) for c in range(CHUNKS)]
    ends = []

    def begin(copy, here):
        if here is None:
            copy.start()
        else:
            pl.when(here)(copy.start)
        ends.append((copy.wait_send, here))

    def finish(wait, here):
        if here is None:
            wait()
        else:
            pl.when(here)(wait)

    if spill:
        first = [
            mover.make(sent.at[peer], from_rows.at[d], (peer, col))
            for d, peer in enumerate(row_peers)
        ]
        for copy in first:
            begin(copy, None)
        downs = [
            mover.make(down.at[:, :, span], got_down.at[:, :, span], (next_row, col))
            for span in spans
        ]
        rights = mover.make(right_rim, got_right, (row, next_col))
        fars = mover.make(far, got_far, (next_row, next_col))
        begin(fars, has_next_far)
        begin(rights, has_next_col)
        for copy in downs:
            begin(copy, has_next_row)
        now[...] = own[...]
        for copy in first:
            copy.wait_recv()
        total = sent[row]
        for d in range(n_row - 1):
            total += from_rows[d]
        from_cols[col] = total
        second = [
            mover.make(from_cols.at[col], from_cols.at[col], (row, peer)) for peer in col_peers
        ]
        for copy in second:
            begin(copy, None)
        finish(rights.wait_recv, has_prev_col)
        finish(fars.wait_recv, has_prev_far)

        @pl.when(has_prev_col)
        def _():
            now[:, :, :edge] -= STEP_OBJECT * got_right[...]

        @pl.when(has_prev_far)
        def _():
            now[:, :edge, :edge] -= STEP_OBJECT * got_far[...]

        for copy in second:
            copy.wait_recv()
        total = from_cols[0]
        for d in range(1, n_col):
            total += from_cols[d]
        per = prb.shape[1]
        out[row] = prb[row] - STEP_PROBE * total[:per] / total[per : per + 1]
        third = [mover.make(out.at[row], out.at[row], (peer, col)) for peer in row_peers]
        for copy in third:
            begin(copy, None)

    if halo:
        ups = [
            mover.make(now.at[:, pl.ds(0, edge), span], below.at[:, :, span], (last_row, col))
            for span in spans
        ]
        lefts = mover.make(now.at[:, :, pl.ds(0, edge)], beside, (row, last_col))
        backs = mover.make(
            now.at[:, pl.ds(0, edge), pl.ds(0, edge)], corner, (last_row, last_col)
        )
    for c in range(CHUNKS):
        if spill:
            finish(downs[c].wait_recv, has_prev_row)

            @pl.when(has_prev_row)
            def _():
                cells = slice(c * step, (c + 1) * step)
                now[:, :edge, cells] -= STEP_OBJECT * got_down[:, :, cells]

        if halo:
            if c == 0:
                begin(backs, has_prev_far)
                begin(lefts, has_prev_col)
            begin(ups[c], has_prev_row)
    if halo:
        finish(backs.wait_recv, has_next_far)
        finish(lefts.wait_recv, has_next_col)
        for copy in ups:
            finish(copy.wait_recv, has_next_row)
    if spill:
        for copy in third:
            copy.wait_recv()
    for wait, here in ends:
        finish(wait, here)


def exchange_call(number, spill, halo, n_row, n_col, edge, own, *rest):
    _, rows, width = own.shape
    vmem = pl.BlockSpec(memory_space=pltpu.VMEM)
    hbm = pl.BlockSpec(memory_space=pl.ANY)
    args, shapes, specs, scratch, count = [own, *rest], [], [], [], 0
    if halo:
        shapes += [(2, edge, width), (2, rows, edge), (2, edge, edge)]
        specs += [hbm] * 3
        count += CHUNKS + 2
    if spill:
        sent, probe = rest[3:]
        args[-1] = probe.reshape(n_row, -1, edge)
        shapes += [own.shape, args[-1].shape]
        specs += [vmem] * 2
        count += CHUNKS + 2 + 2 * (n_row - 1) + n_col - 1
        scratch = [
            (2, edge, width), (2, rows, edge), (2, edge, edge),
            (n_row - 1, *sent.shape[1:]), (n_col, *sent.shape[1:]),
        ]
    results = list(pl.pallas_call(
        functools.partial(exchange_kernel, n_row, n_col, spill, halo),
        out_shape=[jax.ShapeDtypeStruct(shape, jnp.float32) for shape in shapes],
        in_specs=[vmem, hbm, hbm, hbm, vmem, vmem] if spill else [hbm],
        out_specs=specs,
        scratch_shapes=[pltpu.VMEM(shape, jnp.float32) for shape in scratch]
        + [pltpu.SemaphoreType.DMA((count,))] * 2,
        compiler_params=pltpu.CompilerParams(
            collective_id=number, has_side_effects=True, vmem_limit_bytes=24 * 1024 * 1024
        ),
    )(*args))
    if spill:
        results[-1] = results[-1].reshape(probe.shape)
    return results


def body(object_field, probe, position, live_count, intensity):
    side = probe.shape[1]
    n_row, n_col = lax.axis_size("row"), lax.axis_size("col")
    tables = [jnp.asarray(t) for t in fourier_tables(side)]
    places = position[0, 0].reshape(-1)
    measured = intensity[0, 0]
    live = live_count.reshape(1)
    now = object_field
    halos = exchange_call(0, False, True, n_row, n_col, side, now)
    for sweep in range(ITERS):
        parts = slots_call(live, places, now, *halos, probe, tables, measured, n_row)
        more = sweep < ITERS - 1
        *halos, now, probe = exchange_call(
            2 - int(more), True, more, n_row, n_col, side, *parts, probe
        )
    return (now, probe)


def solution(mesh):
    placed = (
        P(None, "row", "col"),
        P(),
        P("row", "col", None, None),
        P("row", "col"),
        P("row", "col", None, None, None),
    )
    return jax.shard_map(
        body, mesh=mesh, in_specs=placed, out_specs=(P(None, "row", "col"), P()), check_vma=False
    )
```

```python
import functools

import jax
import jax.numpy as jnp
import ml_dtypes
import numpy as np
from jax import lax
from jax.experimental import pallas as pl
from jax.experimental.pallas import tpu as pltpu
from jax.sharding import PartitionSpec as P

GROUP = 16
CHAIN = 4
CHUNKS = 4
ITERS = 2
STEP_OBJECT = 0.05
STEP_PROBE = 0.25
MESH = pl.DeviceIdType.MESH


def shifted(block, axis, distance):
    devices = range(lax.axis_size(axis))
    route = [(i - distance, i) for i in devices if i - distance in devices]
    return lax.ppermute(block, axis, route)


def fourier_tables(length):
    indices = np.arange(length)
    angles = (indices[:, None] * indices[None, :] % length) * (2.0 * np.pi / length)
    cos, sin = np.cos(angles), np.sin(angles)
    table = np.block([[cos, sin], [-sin, cos]])

    def parts(full):
        high = full.astype(ml_dtypes.bfloat16)
        low = (full - high.astype(np.float64)).astype(ml_dtypes.bfloat16)
        return high, low

    return (*parts(table), *parts(table.T / length))


def split(value):
    high = value.astype(jnp.bfloat16)
    low = (value - high.astype(jnp.float32)).astype(jnp.bfloat16)
    return high, low


def mm(a, b):
    return jnp.dot(a, b, preferred_element_type=jnp.float32)


def left(table_high, table_low, value):
    high, low = split(value)
    return mm(table_high, high) + mm(table_high, low) + mm(table_low, high)


def right(value, table_high, table_low):
    high, low = split(value)
    return mm(high, table_high) + mm(low, table_high) + mm(high, table_low)


def spectra(waves, wanted, on, a_hi, a_lo, t_hi, t_lo):
    count, side = len(waves), waves[0].shape[0]
    spans = [slice(m * side, (m + 1) * side) for m in range(count)]
    half = right(jnp.concatenate(waves, axis=0), t_hi[...], t_lo[...])
    half = jnp.concatenate(
        [
            jnp.concatenate([half[span, :side] for span in spans], axis=1),
            jnp.concatenate([half[span, side:] for span in spans], axis=1),
        ],
        axis=0,
    )
    far = left(a_hi[...], a_lo[...], half)
    far_re, far_im = far[:side], far[side:]
    power = far_re * far_re + far_im * far_im
    scale = jnp.concatenate(
        [jnp.full((1, side), jnp.where(live, 2.0, 0.0), jnp.float32) for live in on], axis=1
    )
    weight = scale * (power - jnp.concatenate(wanted, axis=1))
    half = left(
        t_hi[...], t_lo[...], jnp.concatenate([weight * far_re, weight * far_im], axis=0)
    )
    half = jnp.concatenate(
        [jnp.concatenate([half[:side, span], half[side:, span]], axis=1) for span in spans],
        axis=0,
    )
    near = right(half, a_hi[...], a_lo[...])
    return [near[span] for span in spans]


def slots_kernel(
    live_ref, pos_ref, own, below, beside, corner, prb_in, tables_in, measured,
    own_out, down_out, right_out, corner_out, pgrad_out,
    ext, grad, pgrad, values, prb, tables, sems,
):
    _, rows, width = own.shape
    side = prb.shape[1]
    strips = width // side
    top, low = pl.ds(0, rows), pl.ds(rows, side)
    copies = [
        pltpu.make_async_copy(measured, values, sems.at[0]),
        pltpu.make_async_copy(prb_in, prb, sems.at[2 * strips + 3]),
        pltpu.make_async_copy(tables_in, tables, sems.at[2 * strips + 4]),
    ]
    a_hi, a_lo, t_hi, t_lo = (tables.at[i] for i in range(4))
    for strip in range(strips):
        columns = pl.ds(strip * side, side)
        copies.append(
            pltpu.make_async_copy(own.at[:, :, columns], ext.at[strip, :, top, :], sems.at[2 * strip + 1])
        )
        copies.append(
            pltpu.make_async_copy(below.at[:, :, columns], ext.at[strip, :, low, :], sems.at[2 * strip + 2])
        )
    copies.append(
        pltpu.make_async_copy(beside, ext.at[strips, :, top, :], sems.at[2 * strips + 1])
    )
    copies.append(
        pltpu.make_async_copy(corner, ext.at[strips, :, low, :], sems.at[2 * strips + 2])
    )
    for copy in copies:
        copy.start()
    for strip in range(strips + 1):
        grad[strip] = jnp.zeros(grad.shape[1:], jnp.float32)
    pgrad[...] = jnp.zeros_like(pgrad)
    for copy in copies:
        copy.wait()

    live = live_ref[0]
    lane = lax.broadcasted_iota(jnp.int32, (side, side), 1)

    def block(index, _):
        places = []
        objects = []
        waves = []
        for member in range(GROUP):
            slot = index * GROUP + member
            on = slot < live
            row = jnp.where(on, pos_ref[2 * slot], 0)
            col = jnp.where(on, pos_ref[2 * slot + 1], 0)
            strip = col // side
            shift = col - strip * side
            keep = lane >= shift
            back = (side - shift) % side
            window = pl.ds(row, side)

            def take(part):
                here = ext[strip, part, window, :]
                there = ext[strip + 1, part, window, :]
                return pltpu.roll(jnp.where(keep, here, there), back, 1)

            obj_re, obj_im = take(0), take(1)
            psi_re = prb[0] * obj_re - prb[1] * obj_im
            psi_im = prb[0] * obj_im + prb[1] * obj_re
            places.append((slot, on, strip, shift, window, keep))
            objects.append((obj_re, obj_im))
            waves.append(jnp.concatenate([psi_re, psi_im], axis=1))
        near = []
        for first in range(0, GROUP, CHAIN):
            members = slice(first, first + CHAIN)
            near += spectra(waves[members], [values[p[0]] for p in places[members]],
                            [p[1] for p in places[members]], a_hi, a_lo, t_hi, t_lo)
        sum_re = jnp.zeros((side, side), jnp.float32)
        sum_im = jnp.zeros((side, side), jnp.float32)
        for member in range(GROUP):
            slot, on, strip, shift, window, keep = places[member]
            obj_re, obj_im = objects[member]
            back_re, back_im = near[member][:, :side], near[member][:, side:]
            sum_re += obj_re * back_re + obj_im * back_im
            sum_im += obj_re * back_im - obj_im * back_re
            for part, value in (
                (0, prb[0] * back_re + prb[1] * back_im),
                (1, prb[0] * back_im - prb[1] * back_re),
            ):
                turned = pltpu.roll(value, shift, 1)
                grad[strip, part, window, :] += jnp.where(keep, turned, 0.0)
                grad[strip + 1, part, window, :] += jnp.where(keep, 0.0, turned)
        pgrad[0] += sum_re
        pgrad[1] += sum_im
        return 0

    lax.fori_loop(0, (live + GROUP - 1) // GROUP, block, 0)

    pieces, deep, _ = pgrad_out.shape
    per = 2 * side // pieces
    for piece in range(pieces):
        part, start = divmod(piece * per, side)
        pgrad_out[piece, :per] = pgrad[part, start : start + per]
        pgrad_out[piece, per:] = jnp.full((deep - per, side), live.astype(jnp.float32))
    copies = []
    for strip in range(strips):
        ext[strip, :, :rows] -= STEP_OBJECT * grad[strip, :, :rows]
        columns = pl.ds(strip * side, side)
        copies.append(
            pltpu.make_async_copy(grad.at[strip, :, low, :], down_out.at[:, :, columns], sems.at[2 * strip])
        )
        copies.append(
            pltpu.make_async_copy(ext.at[strip, :, top, :], own_out.at[:, :, columns], sems.at[2 * strip + 1])
        )
        copies[-2].start()
        copies[-1].start()
    copies.append(
        pltpu.make_async_copy(grad.at[strips, :, top, :], right_out, sems.at[2 * strips])
    )
    copies.append(
        pltpu.make_async_copy(grad.at[strips, :, low, :], corner_out, sems.at[2 * strips + 1])
    )
    copies[-2].start()
    copies[-1].start()
    for copy in copies:
        copy.wait()


def slots_call(live, places, own, below, beside, corner, probe, tables, measured, pieces):
    _, rows, width = own.shape
    side = probe.shape[1]
    strips = width // side
    shape = (strips + 1, 2, rows + side, side)
    smem = pl.BlockSpec(memory_space=pltpu.SMEM)
    vmem = pl.BlockSpec(memory_space=pltpu.VMEM)
    hbm = pl.BlockSpec(memory_space=pl.ANY)
    pinned = pl.BlockSpec(memory_space=pltpu.HBM)
    sent = (pieces, 2 * side // pieces + 8, side)
    return pl.pallas_call(
        slots_kernel,
        out_shape=[
            jax.ShapeDtypeStruct(of, jnp.float32)
            for of in (own.shape, below.shape, beside.shape, corner.shape, sent)
        ],
        in_specs=[smem, smem, hbm, hbm, hbm, hbm, hbm, pinned, pinned],
        out_specs=[hbm, hbm, hbm, hbm, vmem],
        scratch_shapes=[
            pltpu.VMEM(shape, jnp.float32),
            pltpu.VMEM(shape, jnp.float32),
            pltpu.VMEM(probe.shape, jnp.float32),
            pltpu.VMEM(measured.shape, jnp.float32),
            pltpu.VMEM(probe.shape, jnp.float32),
            pltpu.VMEM(tables.shape, tables.dtype),
            pltpu.SemaphoreType.DMA((2 * strips + 5,)),
        ],
        compiler_params=pltpu.CompilerParams(vmem_limit_bytes=40 * 1024 * 1024),
    )(live, places, own, below, beside, corner, probe, tables, measured)


class Mover:
    def __init__(self, sends, recvs):
        self.sends, self.recvs, self.used = sends, recvs, 0

    def make(self, src, dst, peer):
        index, self.used = self.used, self.used + 1
        return pltpu.make_async_remote_copy(
            src_ref=src, dst_ref=dst, send_sem=self.sends.at[index], recv_sem=self.recvs.at[index],
            device_id=peer, device_id_type=MESH,
        )


def exchange_kernel(n_row, n_col, spill, halo, *refs):
    refs = list(refs)
    own = refs.pop(0)
    if spill:
        down, right_rim, far, sent, prb = refs[:5]
        del refs[:5]
    if halo:
        below, beside, corner = refs[:3]
        del refs[:3]
    if spill:
        now, out = refs[:2]
        del refs[:2]
        got_down, got_right, got_far, from_rows, from_cols, head = refs[:6]
        del refs[:6]
    else:
        now = own
    mover = Mover(*refs)
    _, rows, width = now.shape
    row, col = lax.axis_index("row"), lax.axis_index("col")
    row_peers = [lax.rem(row + d, n_row) for d in range(1, n_row)]
    col_peers = [lax.rem(col + d, n_col) for d in range(1, n_col)]
    next_row, last_row = row_peers[0], row_peers[-1]
    next_col, last_col = col_peers[0], col_peers[-1]
    has_prev_row, has_next_row = row > 0, row < n_row - 1
    has_prev_col, has_next_col = col > 0, col < n_col - 1
    passes_corner = jnp.logical_and(has_next_row, has_prev_col)
    takes_corner = jnp.logical_and(has_next_row, has_next_col)

    barrier = pltpu.get_barrier_semaphore()
    greeted = [(peer, col) for peer in row_peers] + [(row, peer) for peer in col_peers]
    for peer in greeted:
        pl.semaphore_signal(barrier, inc=1, device_id=peer, device_id_type=MESH)
    pl.semaphore_wait(barrier, len(greeted))

    edge = corner.shape[1] if halo else far.shape[1]
    step = width // CHUNKS
    spans = [pl.ds(c * step, step) for c in range(CHUNKS)]
    order = [1, 0, *range(2, CHUNKS)] if spill else list(range(CHUNKS))
    ends = []

    def begin(copy, here):
        if here is None:
            copy.start()
        else:
            pl.when(here)(copy.start)
        ends.append((copy.wait_send, here))

    def finish(wait, here):
        if here is None:
            wait()
        else:
            pl.when(here)(wait)

    if spill:
        first = [
            mover.make(sent.at[peer], from_rows.at[d], (peer, col))
            for d, peer in enumerate(row_peers)
        ]
        for copy in first:
            begin(copy, None)
        rights = mover.make(right_rim, got_right, (row, next_col))
        fars = mover.make(far, got_far, (row, next_col))
        begin(fars, has_next_col)
        begin(rights, has_next_col)
        downs = [
            mover.make(
                down.at[:, :, span] if c else head, got_down.at[:, :, span], (next_row, col)
            )
            for c, span in enumerate(spans)
        ]
        begin(downs[1], has_next_row)
        head[...] = down[:, :, :step]
        finish(fars.wait_recv, has_prev_col)

        @pl.when(has_prev_col)
        def _():
            head[:, :, :edge] += got_far[...]

        begin(downs[0], has_next_row)
        now[...] = own[...]
        for copy in first:
            copy.wait_recv()
        total = sent[row]
        for d in range(n_row - 1):
            total += from_rows[d]
        from_cols[col] = total
        second = [
            mover.make(from_cols.at[col], from_cols.at[col], (row, peer)) for peer in col_peers
        ]
        for copy in second:
            begin(copy, None)
        begin(downs[2], has_next_row)
        finish(rights.wait_recv, has_prev_col)

        @pl.when(has_prev_col)
        def _():
            now[:, :, :edge] -= STEP_OBJECT * got_right[...]

    if halo:
        ups = [
            mover.make(now.at[:, pl.ds(0, edge), span], below.at[:, :, span], (last_row, col))
            for span in spans
        ]
        lefts = mover.make(now.at[:, :, pl.ds(0, edge)], beside, (row, last_col))
        passed = mover.make(below.at[:, :, pl.ds(0, edge)], corner, (row, last_col))
    for c in order:
        if spill:
            finish(downs[c].wait_recv, has_prev_row)

            @pl.when(has_prev_row)
            def _():
                cells = slice(c * step, (c + 1) * step)
                now[:, :edge, cells] -= STEP_OBJECT * got_down[:, :, cells]

        if halo:
            if c == 0:
                begin(lefts, has_prev_col)
            begin(ups[c], has_prev_row)
        if spill and c == order[0]:
            for copy in second:
                copy.wait_recv()
            total = from_cols[0]
            for d in range(1, n_col):
                total += from_cols[d]
            per = prb.shape[1]
            out[row] = prb[row] - STEP_PROBE * total[:per] / total[per : per + 1]
            third = [mover.make(out.at[row], out.at[row], (peer, col)) for peer in row_peers]
            for copy in third:
                begin(copy, None)
            for copy in downs[3:]:
                begin(copy, has_next_row)
    if halo:
        finish(ups[0].wait_recv, has_next_row)
        begin(passed, passes_corner)
        finish(lefts.wait_recv, has_next_col)
        for copy in ups[1:]:
            finish(copy.wait_recv, has_next_row)
        finish(passed.wait_recv, takes_corner)
    if spill:
        for copy in third:
            copy.wait_recv()
    for wait, here in ends:
        finish(wait, here)


def exchange_call(number, spill, halo, n_row, n_col, edge, own, *rest):
    _, rows, width = own.shape
    vmem = pl.BlockSpec(memory_space=pltpu.VMEM)
    hbm = pl.BlockSpec(memory_space=pl.ANY)
    pinned = pl.BlockSpec(memory_space=pltpu.HBM)
    args, shapes, specs, scratch, count = [own, *rest], [], [], [], 0
    if halo:
        shapes += [(2, edge, width), (2, rows, edge), (2, edge, edge)]
        specs += [hbm] * 3
        count += CHUNKS + 2
    if spill:
        sent, probe = rest[3:]
        args[-1] = probe.reshape(n_row, -1, edge)
        shapes += [own.shape, args[-1].shape]
        specs += [vmem] * 2
        count += CHUNKS + 2 + 2 * (n_row - 1) + n_col - 1
        scratch = [
            (2, edge, width), (2, rows, edge), (2, edge, edge),
            (n_row - 1, *sent.shape[1:]), (n_col, *sent.shape[1:]), (2, edge, width // CHUNKS),
        ]
    results = list(pl.pallas_call(
        functools.partial(exchange_kernel, n_row, n_col, spill, halo),
        out_shape=[jax.ShapeDtypeStruct(shape, jnp.float32) for shape in shapes],
        in_specs=[vmem, vmem, hbm, hbm, vmem, vmem] if spill else [pinned],
        out_specs=specs,
        scratch_shapes=[pltpu.VMEM(shape, jnp.float32) for shape in scratch]
        + [pltpu.SemaphoreType.DMA((count,))] * 2,
        compiler_params=pltpu.CompilerParams(
            collective_id=number, has_side_effects=True,
            vmem_limit_bytes=(24 if spill else 4) * 1024 * 1024,
        ),
        cost_estimate=pl.CostEstimate(flops=0, transcendentals=0, bytes_accessed=100 * 1024 * 1024),
    )(*args))
    if spill:
        results[-1] = results[-1].reshape(probe.shape)
    return results


def body(object_field, probe, position, live_count, intensity):
    side = probe.shape[1]
    n_row, n_col = lax.axis_size("row"), lax.axis_size("col")
    tables = jnp.asarray(np.stack(fourier_tables(side)))
    places = position[0, 0].reshape(-1)
    measured = intensity[0, 0]
    live = live_count.reshape(1)
    now = object_field
    halos = exchange_call(0, False, True, n_row, n_col, side, now)
    for sweep in range(ITERS):
        parts = slots_call(live, places, now, *halos, probe, tables, measured, n_row)
        more = sweep < ITERS - 1
        *halos, now, probe = exchange_call(
            2 - int(more), True, more, n_row, n_col, side, *parts, probe
        )
    return (now, probe)


def solution(mesh):
    placed = (
        P(None, "row", "col"),
        P(),
        P("row", "col", None, None),
        P("row", "col"),
        P("row", "col", None, None, None),
    )
    return jax.shard_map(
        body, mesh=mesh, in_specs=placed, out_specs=(P(None, "row", "col"), P()), check_vma=False
    )
```

```python
import functools

import jax
import jax.numpy as jnp
import ml_dtypes
import numpy as np
from jax import lax
from jax.experimental import pallas as pl
from jax.experimental.pallas import tpu as pltpu
from jax.sharding import PartitionSpec as P

GROUP = 16
CHAIN = 4
CHUNKS = 4
ITERS = 2
STEP_OBJECT = 0.05
STEP_PROBE = 0.25
MESH = pl.DeviceIdType.MESH


def shifted(block, axis, distance):
    devices = range(lax.axis_size(axis))
    route = [(i - distance, i) for i in devices if i - distance in devices]
    return lax.ppermute(block, axis, route)


def fourier_tables(length):
    indices = np.arange(length)
    angles = (indices[:, None] * indices[None, :] % length) * (2.0 * np.pi / length)
    cos, sin = np.cos(angles), np.sin(angles)
    table = np.block([[cos, sin], [-sin, cos]])

    def parts(full):
        high = full.astype(ml_dtypes.bfloat16)
        low = (full - high.astype(np.float64)).astype(ml_dtypes.bfloat16)
        return high, low

    return (*parts(table), *parts(table.T / length))


def split(value):
    high = value.astype(jnp.bfloat16)
    low = (value - high.astype(jnp.float32)).astype(jnp.bfloat16)
    return high, low


def mm(a, b):
    return jnp.dot(a, b, preferred_element_type=jnp.float32)


def left(table_high, table_low, value):
    high, low = split(value)
    return mm(
        jnp.concatenate([table_high, table_low, table_high], axis=1),
        jnp.concatenate([high, high, low], axis=0),
    )


def right(value, table_high, table_low):
    high, low = split(value)
    return mm(
        jnp.concatenate([high, low, high], axis=1),
        jnp.concatenate([table_high, table_high, table_low], axis=0),
    )


def spectra(waves, wanted, on, a_hi, a_lo, t_hi, t_lo):
    count, side = len(waves), waves[0].shape[0]
    spans = [slice(m * side, (m + 1) * side) for m in range(count)]
    half = right(jnp.concatenate(waves, axis=0), t_hi[...], t_lo[...])
    half = jnp.concatenate(
        [
            jnp.concatenate([half[span, :side] for span in spans], axis=1),
            jnp.concatenate([half[span, side:] for span in spans], axis=1),
        ],
        axis=0,
    )
    far = left(a_hi[...], a_lo[...], half)
    far_re, far_im = far[:side], far[side:]
    power = far_re * far_re + far_im * far_im
    scale = jnp.concatenate(
        [jnp.full((1, side), jnp.where(live, 2.0, 0.0), jnp.float32) for live in on], axis=1
    )
    weight = scale * (power - jnp.concatenate(wanted, axis=1))
    half = left(
        t_hi[...], t_lo[...], jnp.concatenate([weight * far_re, weight * far_im], axis=0)
    )
    half = jnp.concatenate(
        [jnp.concatenate([half[:side, span], half[side:, span]], axis=1) for span in spans],
        axis=0,
    )
    near = right(half, a_hi[...], a_lo[...])
    return [near[span] for span in spans]


def slots_kernel(
    live_ref, pos_ref, own, below, beside, corner, prb_in, tables_in, measured,
    own_out, down_out, right_out, corner_out, pgrad_out,
    ext, grad, pgrad, values, prb, tables, sems,
):
    _, rows, width = own.shape
    side = prb.shape[1]
    strips = width // side
    top, low = pl.ds(0, rows), pl.ds(rows, side)
    copies = [
        pltpu.make_async_copy(measured, values, sems.at[0]),
        pltpu.make_async_copy(prb_in, prb, sems.at[2 * strips + 3]),
        pltpu.make_async_copy(tables_in, tables, sems.at[2 * strips + 4]),
    ]
    a_hi, a_lo, t_hi, t_lo = (tables.at[i] for i in range(4))
    for strip in range(strips):
        columns = pl.ds(strip * side, side)
        copies.append(
            pltpu.make_async_copy(own.at[:, :, columns], ext.at[strip, :, top, :], sems.at[2 * strip + 1])
        )
        copies.append(
            pltpu.make_async_copy(below.at[:, :, columns], ext.at[strip, :, low, :], sems.at[2 * strip + 2])
        )
    copies.append(
        pltpu.make_async_copy(beside, ext.at[strips, :, top, :], sems.at[2 * strips + 1])
    )
    copies.append(
        pltpu.make_async_copy(corner, ext.at[strips, :, low, :], sems.at[2 * strips + 2])
    )
    for copy in copies:
        copy.start()
    for strip in range(strips + 1):
        grad[strip] = jnp.zeros(grad.shape[1:], jnp.float32)
    pgrad[...] = jnp.zeros_like(pgrad)
    for copy in copies:
        copy.wait()

    live = live_ref[0]
    lane = lax.broadcasted_iota(jnp.int32, (side, side), 1)

    def block(index, _):
        places = []
        objects = []
        waves = []
        for member in range(GROUP):
            slot = index * GROUP + member
            on = slot < live
            row = jnp.where(on, pos_ref[2 * slot], 0)
            col = jnp.where(on, pos_ref[2 * slot + 1], 0)
            strip = col // side
            shift = col - strip * side
            keep = lane >= shift
            back = (side - shift) % side
            window = pl.ds(row, side)

            def take(part):
                here = ext[strip, part, window, :]
                there = ext[strip + 1, part, window, :]
                return pltpu.roll(jnp.where(keep, here, there), back, 1)

            obj_re, obj_im = take(0), take(1)
            psi_re = prb[0] * obj_re - prb[1] * obj_im
            psi_im = prb[0] * obj_im + prb[1] * obj_re
            places.append((slot, on, strip, shift, window, keep))
            objects.append((obj_re, obj_im))
            waves.append(jnp.concatenate([psi_re, psi_im], axis=1))
        near = []
        for first in range(0, GROUP, CHAIN):
            members = slice(first, first + CHAIN)
            near += spectra(waves[members], [values[p[0]] for p in places[members]],
                            [p[1] for p in places[members]], a_hi, a_lo, t_hi, t_lo)
        sum_re = jnp.zeros((side, side), jnp.float32)
        sum_im = jnp.zeros((side, side), jnp.float32)
        for member in range(GROUP):
            slot, on, strip, shift, window, keep = places[member]
            obj_re, obj_im = objects[member]
            back_re, back_im = near[member][:, :side], near[member][:, side:]
            sum_re += obj_re * back_re + obj_im * back_im
            sum_im += obj_re * back_im - obj_im * back_re
            for part, value in (
                (0, prb[0] * back_re + prb[1] * back_im),
                (1, prb[0] * back_im - prb[1] * back_re),
            ):
                turned = pltpu.roll(value, shift, 1)
                grad[strip, part, window, :] += jnp.where(keep, turned, 0.0)
                grad[strip + 1, part, window, :] += jnp.where(keep, 0.0, turned)
        pgrad[0] += sum_re
        pgrad[1] += sum_im
        return 0

    lax.fori_loop(0, (live + GROUP - 1) // GROUP, block, 0)

    pieces, deep, _ = pgrad_out.shape
    per = 2 * side // pieces
    for piece in range(pieces):
        part, start = divmod(piece * per, side)
        pgrad_out[piece, :per] = pgrad[part, start : start + per]
        pgrad_out[piece, per:] = jnp.full((deep - per, side), live.astype(jnp.float32))
    copies = []
    for strip in range(strips):
        ext[strip, :, :rows] -= STEP_OBJECT * grad[strip, :, :rows]
        columns = pl.ds(strip * side, side)
        copies.append(
            pltpu.make_async_copy(grad.at[strip, :, low, :], down_out.at[:, :, columns], sems.at[2 * strip])
        )
        copies.append(
            pltpu.make_async_copy(ext.at[strip, :, top, :], own_out.at[:, :, columns], sems.at[2 * strip + 1])
        )
        copies[-2].start()
        copies[-1].start()
    copies.append(
        pltpu.make_async_copy(grad.at[strips, :, top, :], right_out, sems.at[2 * strips])
    )
    copies.append(
        pltpu.make_async_copy(grad.at[strips, :, low, :], corner_out, sems.at[2 * strips + 1])
    )
    copies[-2].start()
    copies[-1].start()
    for copy in copies:
        copy.wait()


def slots_call(live, places, own, below, beside, corner, probe, tables, measured, pieces):
    _, rows, width = own.shape
    side = probe.shape[1]
    strips = width // side
    shape = (strips + 1, 2, rows + side, side)
    smem = pl.BlockSpec(memory_space=pltpu.SMEM)
    vmem = pl.BlockSpec(memory_space=pltpu.VMEM)
    hbm = pl.BlockSpec(memory_space=pl.ANY)
    pinned = pl.BlockSpec(memory_space=pltpu.HBM)
    sent = (pieces, 2 * side // pieces + 8, side)
    return pl.pallas_call(
        slots_kernel,
        out_shape=[
            jax.ShapeDtypeStruct(of, jnp.float32)
            for of in (own.shape, below.shape, beside.shape, corner.shape, sent)
        ],
        in_specs=[smem, smem, hbm, hbm, hbm, hbm, hbm, pinned, pinned],
        out_specs=[hbm, hbm, hbm, hbm, vmem],
        scratch_shapes=[
            pltpu.VMEM(shape, jnp.float32),
            pltpu.VMEM(shape, jnp.float32),
            pltpu.VMEM(probe.shape, jnp.float32),
            pltpu.VMEM(measured.shape, jnp.float32),
            pltpu.VMEM(probe.shape, jnp.float32),
            pltpu.VMEM(tables.shape, tables.dtype),
            pltpu.SemaphoreType.DMA((2 * strips + 5,)),
        ],
        compiler_params=pltpu.CompilerParams(vmem_limit_bytes=40 * 1024 * 1024),
    )(live, places, own, below, beside, corner, probe, tables, measured)


class Mover:
    def __init__(self, sends, recvs):
        self.sends, self.recvs, self.used = sends, recvs, 0

    def make(self, src, dst, peer):
        index, self.used = self.used, self.used + 1
        return pltpu.make_async_remote_copy(
            src_ref=src, dst_ref=dst, send_sem=self.sends.at[index], recv_sem=self.recvs.at[index],
            device_id=peer, device_id_type=MESH,
        )


def exchange_kernel(n_row, n_col, spill, halo, *refs):
    refs = list(refs)
    own = refs.pop(0)
    if spill:
        down, right_rim, far, sent, prb = refs[:5]
        del refs[:5]
    if halo:
        below, beside, corner = refs[:3]
        del refs[:3]
    if spill:
        now, out = refs[:2]
        del refs[:2]
        got_down, got_right, got_far, from_rows, from_cols, head = refs[:6]
        del refs[:6]
    else:
        now = own
    mover = Mover(*refs)
    _, rows, width = now.shape
    row, col = lax.axis_index("row"), lax.axis_index("col")
    row_peers = [lax.rem(row + d, n_row) for d in range(1, n_row)]
    col_peers = [lax.rem(col + d, n_col) for d in range(1, n_col)]
    next_row, last_row = row_peers[0], row_peers[-1]
    next_col, last_col = col_peers[0], col_peers[-1]
    has_prev_row, has_next_row = row > 0, row < n_row - 1
    has_prev_col, has_next_col = col > 0, col < n_col - 1
    passes_corner = jnp.logical_and(has_next_row, has_prev_col)
    takes_corner = jnp.logical_and(has_next_row, has_next_col)

    barrier = pltpu.get_barrier_semaphore()
    greeted = [(peer, col) for peer in row_peers] + [(row, peer) for peer in col_peers]
    for peer in greeted:
        pl.semaphore_signal(barrier, inc=1, device_id=peer, device_id_type=MESH)
    pl.semaphore_wait(barrier, len(greeted))

    edge = corner.shape[1] if halo else far.shape[1]
    step = width // CHUNKS
    spans = [pl.ds(c * step, step) for c in range(CHUNKS)]
    order = [1, 0, *range(2, CHUNKS)] if spill else list(range(CHUNKS))
    ends = []

    def begin(copy, here):
        if here is None:
            copy.start()
        else:
            pl.when(here)(copy.start)
        ends.append((copy.wait_send, here))

    def finish(wait, here):
        if here is None:
            wait()
        else:
            pl.when(here)(wait)

    if spill:
        first = [
            mover.make(sent.at[peer], from_rows.at[d], (peer, col))
            for d, peer in enumerate(row_peers)
        ]
        for copy in first:
            begin(copy, None)
        rights = mover.make(right_rim, got_right, (row, next_col))
        fars = mover.make(far, got_far, (row, next_col))
        begin(fars, has_next_col)
        begin(rights, has_next_col)
        downs = [
            mover.make(
                down.at[:, :, span] if c else head, got_down.at[:, :, span], (next_row, col)
            )
            for c, span in enumerate(spans)
        ]
        begin(downs[1], has_next_row)
        head[...] = down[:, :, :step]
        finish(fars.wait_recv, has_prev_col)

        @pl.when(has_prev_col)
        def _():
            head[:, :, :edge] += got_far[...]

        begin(downs[0], has_next_row)
        now[...] = own[...]
        for copy in first:
            copy.wait_recv()
        total = sent[row]
        for d in range(n_row - 1):
            total += from_rows[d]
        from_cols[col] = total
        second = [
            mover.make(from_cols.at[col], from_cols.at[col], (row, peer)) for peer in col_peers
        ]
        for copy in second:
            begin(copy, None)
        begin(downs[2], has_next_row)
        finish(rights.wait_recv, has_prev_col)

        @pl.when(has_prev_col)
        def _():
            now[:, :, :edge] -= STEP_OBJECT * got_right[...]

    if halo:
        ups = [
            mover.make(now.at[:, pl.ds(0, edge), span], below.at[:, :, span], (last_row, col))
            for span in spans
        ]
        lefts = mover.make(now.at[:, :, pl.ds(0, edge)], beside, (row, last_col))
        passed = mover.make(below.at[:, :, pl.ds(0, edge)], corner, (row, last_col))
    for c in order:
        if spill:
            finish(downs[c].wait_recv, has_prev_row)

            @pl.when(has_prev_row)
            def _():
                cells = slice(c * step, (c + 1) * step)
                now[:, :edge, cells] -= STEP_OBJECT * got_down[:, :, cells]

        if halo:
            if c == 0:
                begin(lefts, has_prev_col)
            begin(ups[c], has_prev_row)
        if spill and c == order[0]:
            for copy in second:
                copy.wait_recv()
            total = from_cols[0]
            for d in range(1, n_col):
                total += from_cols[d]
            per = prb.shape[1]
            out[row] = prb[row] - STEP_PROBE * total[:per] / total[per : per + 1]
            third = [mover.make(out.at[row], out.at[row], (peer, col)) for peer in row_peers]
            for copy in third:
                begin(copy, None)
            for copy in downs[3:]:
                begin(copy, has_next_row)
    if halo:
        finish(ups[0].wait_recv, has_next_row)
        begin(passed, passes_corner)
        finish(lefts.wait_recv, has_next_col)
        for copy in ups[1:]:
            finish(copy.wait_recv, has_next_row)
        finish(passed.wait_recv, takes_corner)
    if spill:
        for copy in third:
            copy.wait_recv()
    for wait, here in ends:
        finish(wait, here)


def exchange_call(number, spill, halo, n_row, n_col, edge, own, *rest):
    _, rows, width = own.shape
    vmem = pl.BlockSpec(memory_space=pltpu.VMEM)
    hbm = pl.BlockSpec(memory_space=pl.ANY)
    pinned = pl.BlockSpec(memory_space=pltpu.HBM)
    args, shapes, specs, scratch, count = [own, *rest], [], [], [], 0
    if halo:
        shapes += [(2, edge, width), (2, rows, edge), (2, edge, edge)]
        specs += [hbm] * 3
        count += CHUNKS + 2
    if spill:
        sent, probe = rest[3:]
        args[-1] = probe.reshape(n_row, -1, edge)
        shapes += [own.shape, args[-1].shape]
        specs += [vmem] * 2
        count += CHUNKS + 2 + 2 * (n_row - 1) + n_col - 1
        scratch = [
            (2, edge, width), (2, rows, edge), (2, edge, edge),
            (n_row - 1, *sent.shape[1:]), (n_col, *sent.shape[1:]), (2, edge, width // CHUNKS),
        ]
    results = list(pl.pallas_call(
        functools.partial(exchange_kernel, n_row, n_col, spill, halo),
        out_shape=[jax.ShapeDtypeStruct(shape, jnp.float32) for shape in shapes],
        in_specs=[vmem, vmem, hbm, hbm, vmem, vmem] if spill else [pinned],
        out_specs=specs,
        scratch_shapes=[pltpu.VMEM(shape, jnp.float32) for shape in scratch]
        + [pltpu.SemaphoreType.DMA((count,))] * 2,
        compiler_params=pltpu.CompilerParams(
            collective_id=number, has_side_effects=True,
            vmem_limit_bytes=(24 if spill else 60) * 1024 * 1024,
        ),
        cost_estimate=pl.CostEstimate(flops=0, transcendentals=0, bytes_accessed=100 * 1024 * 1024),
    )(*args))
    if spill:
        results[-1] = results[-1].reshape(probe.shape)
    return results


def body(object_field, probe, position, live_count, intensity):
    side = probe.shape[1]
    n_row, n_col = lax.axis_size("row"), lax.axis_size("col")
    tables = jnp.asarray(np.stack(fourier_tables(side)))
    places = position[0, 0].reshape(-1)
    measured = intensity[0, 0]
    live = live_count.reshape(1)
    now = object_field
    halos = exchange_call(0, False, True, n_row, n_col, side, now)
    for sweep in range(ITERS):
        parts = slots_call(live, places, now, *halos, probe, tables, measured, n_row)
        more = sweep < ITERS - 1
        *halos, now, probe = exchange_call(
            2 - int(more), True, more, n_row, n_col, side, *parts, probe
        )
    return (now, probe)


def solution(mesh):
    placed = (
        P(None, "row", "col"),
        P(),
        P("row", "col", None, None),
        P("row", "col"),
        P("row", "col", None, None, None),
    )
    return jax.shard_map(
        body, mesh=mesh, in_specs=placed, out_specs=(P(None, "row", "col"), P()), check_vma=False
    )
```

```python
import functools

import jax
import jax.numpy as jnp
import ml_dtypes
import numpy as np
from jax import lax
from jax.experimental import pallas as pl
from jax.experimental.pallas import tpu as pltpu
from jax.sharding import PartitionSpec as P

GROUP = 16
CHAIN = 4
CHUNKS = 4
ITERS = 2
STEP_OBJECT = 0.05
STEP_PROBE = 0.25
MESH = pl.DeviceIdType.MESH


def shifted(block, axis, distance):
    devices = range(lax.axis_size(axis))
    route = [(i - distance, i) for i in devices if i - distance in devices]
    return lax.ppermute(block, axis, route)


def fourier_tables(length):
    indices = np.arange(length)
    angles = (indices[:, None] * indices[None, :] % length) * (2.0 * np.pi / length)
    cos, sin = np.cos(angles), np.sin(angles)
    table = np.block([[cos, sin], [-sin, cos]])

    def parts(full):
        high = full.astype(ml_dtypes.bfloat16)
        low = (full - high.astype(np.float64)).astype(ml_dtypes.bfloat16)
        return high, low

    return (*parts(table), *parts(table.T / length))


def split(value):
    high = value.astype(jnp.bfloat16)
    low = (value - high.astype(jnp.float32)).astype(jnp.bfloat16)
    return high, low


def mm(a, b):
    return jnp.dot(a, b, preferred_element_type=jnp.float32)


def left(table_high, table_low, value):
    high, low = split(value)
    return mm(
        jnp.concatenate([table_high, table_low, table_high], axis=1),
        jnp.concatenate([high, high, low], axis=0),
    )


def right(value, table_high, table_low):
    high, low = split(value)
    return mm(
        jnp.concatenate([high, low, high], axis=1),
        jnp.concatenate([table_high, table_high, table_low], axis=0),
    )


def spectra(waves, wanted, on, a_hi, a_lo, t_hi, t_lo):
    count, side = len(waves), waves[0].shape[0]
    spans = [slice(m * side, (m + 1) * side) for m in range(count)]
    half = right(jnp.concatenate(waves, axis=0), t_hi[...], t_lo[...])
    half = jnp.concatenate(
        [
            jnp.concatenate([half[span, :side] for span in spans], axis=1),
            jnp.concatenate([half[span, side:] for span in spans], axis=1),
        ],
        axis=0,
    )
    far = left(a_hi[...], a_lo[...], half)
    far_re, far_im = far[:side], far[side:]
    power = far_re * far_re + far_im * far_im
    scale = jnp.concatenate(
        [jnp.full((1, side), jnp.where(live, 2.0, 0.0), jnp.float32) for live in on], axis=1
    )
    weight = scale * (power - jnp.concatenate(wanted, axis=1))
    half = left(
        t_hi[...], t_lo[...], jnp.concatenate([weight * far_re, weight * far_im], axis=0)
    )
    half = jnp.concatenate(
        [jnp.concatenate([half[:side, span], half[side:, span]], axis=1) for span in spans],
        axis=0,
    )
    near = right(half, a_hi[...], a_lo[...])
    return [near[span] for span in spans]


def slots_kernel(
    live_ref, pos_ref, own, below, beside, corner, prb_in, tables_in, measured,
    own_out, down_out, right_out, corner_out, pgrad_out,
    ext, grad, pgrad, values, prb, tables, sems,
):
    _, rows, width = own.shape
    side = prb.shape[1]
    strips = width // side
    top, low = pl.ds(0, rows), pl.ds(rows, side)
    copies = [
        pltpu.make_async_copy(measured, values, sems.at[0]),
        pltpu.make_async_copy(prb_in, prb, sems.at[2 * strips + 3]),
        pltpu.make_async_copy(tables_in, tables, sems.at[2 * strips + 4]),
    ]
    a_hi, a_lo, t_hi, t_lo = (tables.at[i] for i in range(4))
    for strip in range(strips):
        columns = pl.ds(strip * side, side)
        copies.append(
            pltpu.make_async_copy(own.at[:, :, columns], ext.at[strip, :, top, :], sems.at[2 * strip + 1])
        )
        copies.append(
            pltpu.make_async_copy(below.at[:, :, columns], ext.at[strip, :, low, :], sems.at[2 * strip + 2])
        )
    copies.append(
        pltpu.make_async_copy(beside, ext.at[strips, :, top, :], sems.at[2 * strips + 1])
    )
    copies.append(
        pltpu.make_async_copy(corner, ext.at[strips, :, low, :], sems.at[2 * strips + 2])
    )
    for copy in copies:
        copy.start()
    for strip in range(strips + 1):
        grad[strip] = jnp.zeros(grad.shape[1:], jnp.float32)
    pgrad[...] = jnp.zeros_like(pgrad)
    for copy in copies:
        copy.wait()

    live = live_ref[0]
    lane = lax.broadcasted_iota(jnp.int32, (side, side), 1)

    def block(index, _):
        places = []
        objects = []
        waves = []
        for member in range(GROUP):
            slot = index * GROUP + member
            on = slot < live
            row = jnp.where(on, pos_ref[2 * slot], 0)
            col = jnp.where(on, pos_ref[2 * slot + 1], 0)
            strip = col // side
            shift = col - strip * side
            keep = lane >= shift
            back = (side - shift) % side
            window = pl.ds(row, side)

            def take(part):
                here = ext[strip, part, window, :]
                there = ext[strip + 1, part, window, :]
                return pltpu.roll(jnp.where(keep, here, there), back, 1)

            obj_re, obj_im = take(0), take(1)
            psi_re = prb[0] * obj_re - prb[1] * obj_im
            psi_im = prb[0] * obj_im + prb[1] * obj_re
            places.append((slot, on, strip, shift, window, keep))
            objects.append((obj_re, obj_im))
            waves.append(jnp.concatenate([psi_re, psi_im], axis=1))
        near = []
        for first in range(0, GROUP, CHAIN):
            members = slice(first, first + CHAIN)
            near += spectra(waves[members], [values[p[0]] for p in places[members]],
                            [p[1] for p in places[members]], a_hi, a_lo, t_hi, t_lo)
        sum_re = jnp.zeros((side, side), jnp.float32)
        sum_im = jnp.zeros((side, side), jnp.float32)
        for member in range(GROUP):
            slot, on, strip, shift, window, keep = places[member]
            obj_re, obj_im = objects[member]
            back_re, back_im = near[member][:, :side], near[member][:, side:]
            sum_re += obj_re * back_re + obj_im * back_im
            sum_im += obj_re * back_im - obj_im * back_re
            for part, value in (
                (0, prb[0] * back_re + prb[1] * back_im),
                (1, prb[0] * back_im - prb[1] * back_re),
            ):
                turned = pltpu.roll(value, shift, 1)
                grad[strip, part, window, :] += jnp.where(keep, turned, 0.0)
                grad[strip + 1, part, window, :] += jnp.where(keep, 0.0, turned)
        pgrad[0] += sum_re
        pgrad[1] += sum_im
        return 0

    lax.fori_loop(0, (live + GROUP - 1) // GROUP, block, 0)

    pieces, deep, _ = pgrad_out.shape
    per = 2 * side // pieces
    for piece in range(pieces):
        part, start = divmod(piece * per, side)
        pgrad_out[piece, :per] = pgrad[part, start : start + per]
        pgrad_out[piece, per:] = jnp.full((deep - per, side), live.astype(jnp.float32))
    copies = []
    for strip in range(strips):
        ext[strip, :, :rows] -= STEP_OBJECT * grad[strip, :, :rows]
        columns = pl.ds(strip * side, side)
        copies.append(
            pltpu.make_async_copy(grad.at[strip, :, low, :], down_out.at[:, :, columns], sems.at[2 * strip])
        )
        copies.append(
            pltpu.make_async_copy(ext.at[strip, :, top, :], own_out.at[:, :, columns], sems.at[2 * strip + 1])
        )
        copies[-2].start()
        copies[-1].start()
    copies.append(
        pltpu.make_async_copy(grad.at[strips, :, top, :], right_out, sems.at[2 * strips])
    )
    copies.append(
        pltpu.make_async_copy(grad.at[strips, :, low, :], corner_out, sems.at[2 * strips + 1])
    )
    copies[-2].start()
    copies[-1].start()
    for copy in copies:
        copy.wait()


def slots_call(live, places, own, below, beside, corner, probe, tables, measured, pieces):
    _, rows, width = own.shape
    side = probe.shape[1]
    strips = width // side
    shape = (strips + 1, 2, rows + side, side)
    smem = pl.BlockSpec(memory_space=pltpu.SMEM)
    vmem = pl.BlockSpec(memory_space=pltpu.VMEM)
    hbm = pl.BlockSpec(memory_space=pl.ANY)
    pinned = pl.BlockSpec(memory_space=pltpu.HBM)
    sent = (pieces, 2 * side // pieces + 8, side)
    return pl.pallas_call(
        slots_kernel,
        out_shape=[
            jax.ShapeDtypeStruct(of, jnp.float32)
            for of in (own.shape, below.shape, beside.shape, corner.shape, sent)
        ],
        in_specs=[smem, smem, hbm, hbm, hbm, hbm, hbm, pinned, pinned],
        out_specs=[hbm, hbm, hbm, hbm, vmem],
        scratch_shapes=[
            pltpu.VMEM(shape, jnp.float32),
            pltpu.VMEM(shape, jnp.float32),
            pltpu.VMEM(probe.shape, jnp.float32),
            pltpu.VMEM(measured.shape, jnp.float32),
            pltpu.VMEM(probe.shape, jnp.float32),
            pltpu.VMEM(tables.shape, tables.dtype),
            pltpu.SemaphoreType.DMA((2 * strips + 5,)),
        ],
        compiler_params=pltpu.CompilerParams(vmem_limit_bytes=60 * 1024 * 1024),
    )(live, places, own, below, beside, corner, probe, tables, measured)


class Mover:
    def __init__(self, sends, recvs):
        self.sends, self.recvs, self.used = sends, recvs, 0

    def make(self, src, dst, peer):
        index, self.used = self.used, self.used + 1
        return pltpu.make_async_remote_copy(
            src_ref=src, dst_ref=dst, send_sem=self.sends.at[index], recv_sem=self.recvs.at[index],
            device_id=peer, device_id_type=MESH,
        )


def exchange_kernel(n_row, n_col, spill, halo, *refs):
    refs = list(refs)
    own = refs.pop(0)
    if spill:
        down, right_rim, far, sent, prb = refs[:5]
        del refs[:5]
    if halo:
        below, beside, corner = refs[:3]
        del refs[:3]
    if spill:
        now, out = refs[:2]
        del refs[:2]
        got_down, got_right, got_far, from_rows, from_cols, head, mine, prb_mine = refs[:8]
        local = refs.pop()
        del refs[:8]
    else:
        now = own
    mover = Mover(*refs)
    _, rows, width = now.shape
    row, col = lax.axis_index("row"), lax.axis_index("col")
    row_peers = [lax.rem(row + d, n_row) for d in range(1, n_row)]
    col_peers = [lax.rem(col + d, n_col) for d in range(1, n_col)]
    next_row, last_row = row_peers[0], row_peers[-1]
    next_col, last_col = col_peers[0], col_peers[-1]
    has_prev_row, has_next_row = row > 0, row < n_row - 1
    has_prev_col, has_next_col = col > 0, col < n_col - 1
    passes_corner = jnp.logical_and(has_next_row, has_prev_col)
    takes_corner = jnp.logical_and(has_next_row, has_next_col)

    if spill:
        step = now.shape[2] // CHUNKS
        fetches = [
            pltpu.make_async_copy(down.at[:, :, pl.ds(0, step)], head, local.at[0]),
            pltpu.make_async_copy(sent.at[row], mine, local.at[1]),
            pltpu.make_async_copy(prb.at[row], prb_mine, local.at[2]),
            pltpu.make_async_copy(own, now, local.at[3]),
        ]
        for copy in fetches:
            copy.start()

    barrier = pltpu.get_barrier_semaphore()
    greeted = [(peer, col) for peer in row_peers] + [(row, peer) for peer in col_peers]
    for peer in greeted:
        pl.semaphore_signal(barrier, inc=1, device_id=peer, device_id_type=MESH)
    pl.semaphore_wait(barrier, len(greeted))

    edge = corner.shape[1] if halo else far.shape[1]
    step = width // CHUNKS
    spans = [pl.ds(c * step, step) for c in range(CHUNKS)]
    order = [1, 0, *range(2, CHUNKS)] if spill else list(range(CHUNKS))
    ends = []

    def begin(copy, here):
        if here is None:
            copy.start()
        else:
            pl.when(here)(copy.start)
        ends.append((copy.wait_send, here))

    def finish(wait, here):
        if here is None:
            wait()
        else:
            pl.when(here)(wait)

    if spill:
        first = [
            mover.make(sent.at[peer], from_rows.at[d], (peer, col))
            for d, peer in enumerate(row_peers)
        ]
        for copy in first:
            begin(copy, None)
        rights = mover.make(right_rim, got_right, (row, next_col))
        fars = mover.make(far, got_far, (row, next_col))
        begin(fars, has_next_col)
        begin(rights, has_next_col)
        downs = [
            mover.make(
                down.at[:, :, span] if c else head, got_down.at[:, :, span], (next_row, col)
            )
            for c, span in enumerate(spans)
        ]
        begin(downs[1], has_next_row)
        for copy in fetches:
            copy.wait()
        finish(fars.wait_recv, has_prev_col)

        @pl.when(has_prev_col)
        def _():
            head[:, :, :edge] += got_far[...]

        begin(downs[0], has_next_row)
        for copy in first:
            copy.wait_recv()
        total = mine[...]
        for d in range(n_row - 1):
            total += from_rows[d]
        from_cols[col] = total
        second = [
            mover.make(from_cols.at[col], from_cols.at[col], (row, peer)) for peer in col_peers
        ]
        for copy in second:
            begin(copy, None)
        begin(downs[2], has_next_row)
        finish(rights.wait_recv, has_prev_col)

        @pl.when(has_prev_col)
        def _():
            now[:, :, :edge] -= STEP_OBJECT * got_right[...]

    if halo:
        ups = [
            mover.make(now.at[:, pl.ds(0, edge), span], below.at[:, :, span], (last_row, col))
            for span in spans
        ]
        lefts = mover.make(now.at[:, :, pl.ds(0, edge)], beside, (row, last_col))
        passed = mover.make(below.at[:, :, pl.ds(0, edge)], corner, (row, last_col))
    for c in order:
        if spill:
            finish(downs[c].wait_recv, has_prev_row)

            @pl.when(has_prev_row)
            def _():
                cells = slice(c * step, (c + 1) * step)
                now[:, :edge, cells] -= STEP_OBJECT * got_down[:, :, cells]

        if halo:
            if c == 0:
                begin(lefts, has_prev_col)
            begin(ups[c], has_prev_row)
        if spill and c == order[0]:
            for copy in second:
                copy.wait_recv()
            total = from_cols[0]
            for d in range(1, n_col):
                total += from_cols[d]
            per = prb.shape[1]
            out[row] = prb_mine[...] - STEP_PROBE * total[:per] / total[per : per + 1]
            third = [mover.make(out.at[row], out.at[row], (peer, col)) for peer in row_peers]
            for copy in third:
                begin(copy, None)
            for copy in downs[3:]:
                begin(copy, has_next_row)
    if halo:
        finish(ups[0].wait_recv, has_next_row)
        begin(passed, passes_corner)
        finish(lefts.wait_recv, has_next_col)
        for copy in ups[1:]:
            finish(copy.wait_recv, has_next_row)
        finish(passed.wait_recv, takes_corner)
    if spill:
        for copy in third:
            copy.wait_recv()
    for wait, here in ends:
        finish(wait, here)


def exchange_call(number, spill, halo, n_row, n_col, edge, own, *rest):
    _, rows, width = own.shape
    vmem = pl.BlockSpec(memory_space=pltpu.VMEM)
    hbm = pl.BlockSpec(memory_space=pl.ANY)
    args, shapes, specs, scratch, count = [own, *rest], [], [], [], 0
    if halo:
        shapes += [(2, edge, width), (2, rows, edge), (2, edge, edge)]
        specs += [hbm] * 3
        count += CHUNKS + 2
    if spill:
        sent, probe = rest[3:]
        args[-1] = probe.reshape(n_row, -1, edge)
        shapes += [own.shape, args[-1].shape]
        specs += [vmem] * 2
        count += CHUNKS + 2 + 2 * (n_row - 1) + n_col - 1
        scratch = [
            (2, edge, width), (2, rows, edge), (2, edge, edge),
            (n_row - 1, *sent.shape[1:]), (n_col, *sent.shape[1:]), (2, edge, width // CHUNKS),
            sent.shape[1:], args[-1].shape[1:],
        ]
    results = list(pl.pallas_call(
        functools.partial(exchange_kernel, n_row, n_col, spill, halo),
        out_shape=[jax.ShapeDtypeStruct(shape, jnp.float32) for shape in shapes],
        in_specs=[hbm] * len(args),
        out_specs=specs,
        scratch_shapes=[pltpu.VMEM(shape, jnp.float32) for shape in scratch]
        + [pltpu.SemaphoreType.DMA((count,))] * 2
        + [pltpu.SemaphoreType.DMA((4,))] * int(spill),
        compiler_params=pltpu.CompilerParams(
            collective_id=number, has_side_effects=True,
            vmem_limit_bytes=60 * 1024 * 1024,
        ),
        cost_estimate=pl.CostEstimate(flops=0, transcendentals=0, bytes_accessed=100 * 1024 * 1024),
    )(*args))
    if spill:
        results[-1] = results[-1].reshape(probe.shape)
    return results


def body(object_field, probe, position, live_count, intensity):
    side = probe.shape[1]
    n_row, n_col = lax.axis_size("row"), lax.axis_size("col")
    tables = jnp.asarray(np.stack(fourier_tables(side)))
    places = position[0, 0].reshape(-1)
    measured = intensity[0, 0]
    live = live_count.reshape(1)
    now = object_field
    halos = exchange_call(0, False, True, n_row, n_col, side, now)
    for sweep in range(ITERS):
        parts = slots_call(live, places, now, *halos, probe, tables, measured, n_row)
        more = sweep < ITERS - 1
        *halos, now, probe = exchange_call(
            2 - int(more), True, more, n_row, n_col, side, *parts, probe
        )
    return (now, probe)


def solution(mesh):
    placed = (
        P(None, "row", "col"),
        P(),
        P("row", "col", None, None),
        P("row", "col"),
        P("row", "col", None, None, None),
    )
    return jax.shard_map(
        body, mesh=mesh, in_specs=placed, out_specs=(P(None, "row", "col"), P()), check_vma=False
    )
```
